32 devices in a mesh: group: 2 (over x), prow: 8 (over z, y), pcol: 2 (over core).
Axes of the slice: x: 2, y: 2, z: 4, core: 2. Of those that a mesh axis runs over, the one named last changes fastest.
Arguments:
- orbitals: bfloat16 [32768, 1024], P(('group', 'prow', 'pcol')), parts along dimension 0, may hold values from -6 to 6
- points: int32 [4096], P(('group', 'prow', 'pcol')), parts along dimension 0, may hold values from 0 to 1023, as said below
- kernel: bfloat16 [4096, 8, 2, 128], P(('group', 'prow'), None, 'pcol'), parts along dimension 0, may hold values from -0.009765625 to 0.009765625
Outputs:
- exchange: bfloat16 [4096, 1024], P(('group', 'prow'), 'pcol'), parts along dimension 0
The draws below stay inside these ranges and needn't reach their ends.
There are 2 independent parts, one for each index of `group`. The reference program is written for one: setup_inputs(seed, part) draws one part's arguments, and reference() takes and returns one part's arrays. A program takes and returns all parts, laid end to end along the dimension named above; each array names one. Nothing has to cross between parts.
Inputs may be any that keep to these rules, and one draw needn't show every extreme that they name: Within one block of 128 consecutive points the values are distinct; value v in block b names grid row b * 1024 + v.
All inputs are finite; a program needn't handle non-finite values.
Results may differ from the reference program's by a relative error of at most 0.0051.
Values may be sent and summed in bfloat16 or wider, within the bound.
A program may use at most 128 MiB of HBM per device.

```python
import math
import jax
import jax.numpy as jnp
from jax import lax

PTS_DEV = 128
NOCC = 1024
G_DEV = 1024
MU = 2048
NGRID = 16384
N_PROW = 8
N_PCOL = 2


def draw_points(key, part):
    key = jax.random.fold_in(key, 11)
    block_count = MU // PTS_DEV
    block_keys = jax.random.split(key, block_count)

    def one_block(block_key):
        first_key, second_key = jax.random.split(block_key)
        inner = jax.random.permutation(first_key, jnp.arange(1, G_DEV - 1, dtype=jnp.int32))[:PTS_DEV - 2]
        chosen = jnp.concatenate([jnp.array([0, G_DEV - 1], dtype=jnp.int32), inner])
        return jax.random.permutation(second_key, chosen)
    return jax.vmap(one_block)(block_keys).reshape(MU).astype(jnp.int32)


def block_scale(stream_key, dims, shards, least, high):
    factor_of, own = 1.0, jax.random.fold_in(stream_key, 6)
    for dim, shards_of in shards:
        draws = jnp.exp(jax.random.uniform(jax.random.fold_in(own, dim), (shards_of,), jnp.float32, least / len(shards), high / len(shards)))
        factor_of = factor_of * jnp.repeat(draws, dims[dim] // shards_of).reshape([-1 if axis == dim else 1 for axis in range(len(dims))])
    return factor_of


def noise(own_key, shape, scale, most, cuts=(), kind=jnp.bfloat16):
    factor_of = block_scale(own_key, shape, cuts, -0.22, 0.18) if cuts else 1.0
    values = jax.random.normal(own_key, shape, jnp.float32) * scale * factor_of
    return jnp.minimum(jnp.maximum(values, -most), most).astype(kind)


def setup_inputs(seed: int = 0, part: int = 0) -> dict:
    key_list = jax.random.split(jax.random.key(seed), 4)
    own_keys = jax.random.split(jax.random.fold_in(key_list[3], part), 4)
    return {
        "orbitals": noise(own_keys[0], (NGRID, NOCC), 1.0, 6.0, ((0, 16),)),
        "points": draw_points(jax.random.fold_in(jax.random.fold_in(key_list[3], part), 71), part),
        "kernel": noise(own_keys[2], (MU, N_PROW, N_PCOL, PTS_DEV), (1.0 / (MU * NOCC) ** 0.5), 0.009765625, ((0, 8), (2, 2))),
    }


def reference(orbitals, points, kernel):
    blocks = jnp.arange(MU, dtype=jnp.int32) // PTS_DEV
    grid_rows = (blocks * G_DEV + points).astype(jnp.int32)
    values = jnp.take(orbitals, grid_rows, axis=0)
    flat = kernel.reshape(MU, MU)
    step_rows = math.gcd(MU, 512)

    def one_block(begin):
        value_rows = lax.dynamic_slice_in_dim(values, begin, step_rows, 0)
        kernel_rows = lax.dynamic_slice_in_dim(flat, begin, step_rows, 0)
        density = lax.dot_general(value_rows, values, (((1,), (1,)), ((), ())), preferred_element_type=jnp.float32)
        screened = (kernel_rows.astype(jnp.float32) * density).astype(jnp.bfloat16)
        return jnp.dot(screened, values, preferred_element_type=jnp.float32).astype(jnp.bfloat16)

    starts = jnp.arange(0, MU, step_rows, dtype=jnp.int32)
    result = lax.map(one_block, starts)
    return result.reshape(MU, NOCC)
```

```python
import functools

import jax
import jax.numpy as jnp
from jax import lax
from jax.experimental import pallas as pl
from jax.experimental.pallas import tpu as pltpu
from jax.sharding import PartitionSpec as P

MESH = pl.DeviceIdType.MESH
CH = 4
HALF = CH // 2


def ring_index(pos, n):
    return jnp.where(pos < n // 2, 2 * pos, 2 * (n - 1 - pos) + 1)


def dot(a, b):
    return jnp.dot(a, b, preferred_element_type=jnp.float32)


def dot_t(a, b):
    return lax.dot_general(a, b, (((1,), (1,)), ((), ())), preferred_element_type=jnp.float32)


def body(
    n, orb_hbm, pts_ref, ker_hbm, out_ref,
    orb, ker, ker32, rows, blocks, sib_blocks, scr, sib_scr, acc,
    orb_sem, ker_sem, row_send, row_recv, ring_send, ring_recv, blk_send, blk_recv, scr_send, scr_recv,
):
    last = n // 2
    pts = pts_ref.shape[1]
    grid_rows, wide = orb.shape[1], orb.shape[2]
    group, prow, core = lax.axis_index("group"), lax.axis_index("prow"), lax.axis_index("pcol")
    pos = jnp.where(prow % 2 == 0, prow // 2, n - 1 - prow // 2)
    right = (group, ring_index((pos + 1) % n, n), core)
    left = (group, ring_index((pos + n - 1) % n, n), core)
    sibling = (group, prow, 1 - core)
    mine = pl.ds(pl.multiple_of(core * pts, pts), pts)
    theirs = pl.ds(pl.multiple_of((1 - core) * pts, pts), pts)
    side = (pl.ds(0, pts), pl.ds(pts, pts))

    def remote(src, dst, send, recv, device):
        return pltpu.make_async_remote_copy(
            src_ref=src, dst_ref=dst, send_sem=send, recv_sem=recv, device_id=device, device_id_type=MESH
        )

    def hop(way, s, c):
        static_first = isinstance(s, int) and s == 0
        static_last = isinstance(s, int) and s == last - 1
        src = rows.at[c, mine] if static_first else blocks.at[s, c, side[way]]
        dst = blocks.at[s + 1, c, side[0] if static_last else side[way]]
        return remote(
            src, dst, ring_send.at[way, s, c], ring_recv.at[way, s + 1, c], right if way == 0 else left
        )

    def row_copy(c):
        return remote(rows.at[c, mine], rows.at[c, mine], row_send.at[c], row_recv.at[c], sibling)

    def row_arrival(c):
        return remote(rows.at[c, theirs], rows.at[c, theirs], row_send.at[c], row_recv.at[c], sibling)

    def blk_copy(s, at_last=False):
        far = pl.ds((1 - core) * HALF, HALF)
        if at_last:
            return remote(
                blocks.at[s, far, side[0]], sib_blocks.at[s, :, side[0]], blk_send.at[s], blk_recv.at[s], sibling
            )
        return remote(blocks.at[s, far], sib_blocks.at[s], blk_send.at[s], blk_recv.at[s], sibling)

    def scr_copy(s, narrow=False):
        if narrow:
            return remote(
                scr.at[s, :, side[0]], sib_scr.at[s, :, side[0]], scr_send.at[s], scr_recv.at[s], sibling
            )
        return remote(scr.at[s], sib_scr.at[s], scr_send.at[s], scr_recv.at[s], sibling)

    def kernel_columns(index):
        return ker32[pl.ds(index, out_ref.shape[0], stride=n), :]

    order = (0, 2, 1, 3)
    loads = [
        pltpu.make_async_copy(orb_hbm.at[:, pl.ds(c * wide, wide)], orb.at[c], orb_sem.at[c]) for c in range(CH)
    ]
    for c in order:
        loads[c].start()
    ker_load = pltpu.make_async_copy(ker_hbm, ker, ker_sem)
    ker_load.start()

    barrier = pltpu.get_barrier_semaphore()
    for device in (left, right, sibling):
        pl.semaphore_signal(barrier, inc=1, device_id=device, device_id_type=MESH)

    wanted = jnp.transpose(jnp.broadcast_to(pts_ref[...], (pts, pts)))
    wanted = jnp.concatenate([wanted] * (grid_rows // pts), axis=1)
    hot = (wanted == lax.broadcasted_iota(jnp.int32, (pts, grid_rows), 1)).astype(jnp.float32).astype(jnp.bfloat16)

    for k, c in enumerate(order):
        loads[c].wait()
        rows[c, mine] = dot(hot, orb[c]).astype(jnp.bfloat16)
        if k == 0:
            pl.semaphore_wait(barrier, 3)
        hop(0 if c < HALF else 1, 0, c).start()
        row_copy(c).start()
    for c in range(HALF):
        hop(0, 0, c + HALF).start()
        hop(1, 0, c).start()

    ker_load.wait()
    ker32[...] = ker[...].astype(jnp.float32).reshape(ker32.shape)

    for c in range(CH):
        row_arrival(c).wait_recv()
    density = dot_t(rows[0], rows[0, mine])
    for c in range(1, CH):
        density += dot_t(rows[c], rows[c, mine])
    screened = (kernel_columns(prow) * density).astype(jnp.bfloat16)
    scr[0, :, side[0]] = screened
    scr_copy(0, True).start()
    for i in range(HALF):
        acc[i] = dot(screened, rows[core * HALF + i, mine])

    def late(s):
        scr_copy(s).wait_recv()
        blk_copy(s).wait_recv()
        for i in range(HALF):
            acc[i] += dot(sib_scr[s], sib_blocks[s, i])

    def late_first():
        scr_copy(0, True).wait_recv()
        for i in range(HALF):
            acc[i] += dot(sib_scr[0, :, side[0]], rows[core * HALF + i, theirs])

    def step(s):
        for k in range(CH):
            for way in (0, 1):
                c = (k + way * HALF) % CH
                hop(way, s - 1, c).wait_recv()
                if not isinstance(s, int) or s < last - 1 or k < HALF:
                    hop(way, s, c).start()
        blk_copy(s).start()
        density = dot_t(rows[0], blocks[s, 0])
        for c in range(1, CH):
            density += dot_t(rows[c], blocks[s, c])
        from_left = kernel_columns(ring_index((pos + n - s) % n, n))
        from_right = kernel_columns(ring_index((pos + s) % n, n))
        screened = (jnp.concatenate([from_left, from_right], axis=1) * density).astype(jnp.bfloat16)
        scr[s] = screened
        scr_copy(s).start()
        for i in range(HALF):
            acc[i] += dot(screened, blocks[s, core * HALF + i])

    step(1)
    late_first()

    if last == 4:
        step(2)
        late(1)
    else:

        @pl.loop(2, last - 1)
        def _(s):
            step(s)
            late(s - 1)

    step(last - 1)
    late(last - 2)

    far = side[0]
    for k in range(HALF):
        hop(0, last - 1, k).wait_recv()
        hop(1, last - 1, k + HALF).wait_recv()
        part = dot_t(rows[k], blocks[last, k, far]) + dot_t(rows[k + HALF], blocks[last, k + HALF, far])
        density = part if k == 0 else density + part
    blk_copy(last, True).start()
    screened = (kernel_columns(ring_index((pos + last) % n, n)) * density).astype(jnp.bfloat16)
    scr[last, :, far] = screened
    scr_copy(last, True).start()
    late(last - 1)
    for i in range(HALF):
        acc[i] += dot(screened, blocks[last, core * HALF + i, far])
    blk_copy(last, True).wait_recv()
    scr_copy(last, True).wait_recv()
    for i in range(HALF):
        total = acc[i] + dot(sib_scr[last, :, far], sib_blocks[last, i, far])
        out_ref[:, pl.ds(i * wide, wide)] = total.astype(out_ref.dtype)

    for c in range(CH):
        row_copy(c).wait_send()
        for way in (0, 1):
            hop(way, 0, c).wait_send()
            hop(way, 1, c).wait_send()

    def drain(s):
        for c in range(CH):
            for way in (0, 1):
                hop(way, s, c).wait_send()

    if last == 4:
        drain(2)
    else:
        pl.loop(2, last - 1)(drain)
    for k in range(HALF):
        hop(0, last - 1, k).wait_send()
        hop(1, last - 1, k + HALF).wait_send()
    scr_copy(0, True).wait_send()
    scr_copy(last, True).wait_send()
    blk_copy(last, True).wait_send()

    def drain_pair(s):
        scr_copy(s).wait_send()
        blk_copy(s).wait_send()

    if last == 4:
        for s in range(1, last):
            drain_pair(s)
    else:
        pl.loop(1, last)(drain_pair)


def shards(n, orbitals, points, kernel):
    grid_rows, nocc = orbitals.shape
    pts = points.shape[0]
    row_total = kernel.shape[0]
    wide = nocc // CH
    slots = n // 2 + 1
    bf16, f32 = jnp.bfloat16, jnp.float32
    dma = pltpu.SemaphoreType.DMA
    scratch = [
        pltpu.VMEM((CH, grid_rows, wide), bf16),
        pltpu.VMEM((row_total, n, pts), bf16),
        pltpu.VMEM((row_total * n, pts), f32),
        pltpu.VMEM((CH, row_total, wide), bf16),
        pltpu.VMEM((slots, CH, 2 * pts, wide), bf16),
        pltpu.VMEM((slots, HALF, 2 * pts, wide), bf16),
        pltpu.VMEM((slots, row_total, 2 * pts), bf16),
        pltpu.VMEM((slots, row_total, 2 * pts), bf16),
        pltpu.VMEM((HALF, row_total, wide), f32),
        dma((CH,)),
        dma,
        dma((CH,)),
        dma((CH,)),
        dma((2, slots, CH)),
        dma((2, slots, CH)),
        dma((slots,)),
        dma((slots,)),
        dma((slots,)),
        dma((slots,)),
    ]
    flops = 4 * row_total * n * pts * nocc
    return pl.pallas_call(
        functools.partial(body, n),
        out_shape=jax.ShapeDtypeStruct((row_total, nocc // 2), bf16),
        in_specs=[
            pl.BlockSpec(memory_space=pl.ANY),
            pl.BlockSpec(memory_space=pltpu.VMEM),
            pl.BlockSpec(memory_space=pl.ANY),
        ],
        out_specs=pl.BlockSpec(memory_space=pltpu.VMEM),
        scratch_shapes=scratch,
        compiler_params=pltpu.CompilerParams(
            collective_id=0, has_side_effects=True, vmem_limit_bytes=(20 if n <= 8 else 58) * 2**20
        ),
        cost_estimate=pl.CostEstimate(flops=flops, bytes_accessed=orbitals.size * 2, transcendentals=0),
    )(orbitals, points.reshape(1, pts), kernel.reshape(row_total, n, pts))


def solution(mesh):
    in_specs = (
        P(("group", "prow", "pcol"), None),
        P(("group", "prow", "pcol")),
        P(("group", "prow"), None, "pcol", None),
    )
    out_specs = P(("group", "prow"), "pcol")
    return jax.shard_map(
        functools.partial(shards, mesh.shape["prow"]),
        mesh=mesh, in_specs=in_specs, out_specs=out_specs, check_vma=False,
    )
```

```python
import functools

import jax
import jax.numpy as jnp
from jax import lax
from jax.experimental import pallas as pl
from jax.experimental.pallas import tpu as pltpu
from jax.sharding import PartitionSpec as P

MESH = pl.DeviceIdType.MESH
CH = 4
HALF = CH // 2


def ring_index(pos, n):
    return jnp.where(pos < n // 2, 2 * pos, 2 * (n - 1 - pos) + 1)


def dot(a, b):
    return jnp.dot(a, b, preferred_element_type=jnp.float32)


def dot_t(a, b):
    return lax.dot_general(a, b, (((1,), (1,)), ((), ())), preferred_element_type=jnp.float32)


def body(
    n, orb_hbm, pts_hbm, ker_hbm, out_ref,
    pts_ref, orb, ker, ker32, rows, blocks, sib_blocks, scr, sib_scr, acc,
    pts_sem, orb_sem, ker_sem, row_send, row_recv, ring_send, ring_recv, blk_send, blk_recv, scr_send, scr_recv,
):
    last = n // 2
    pts = pts_ref.shape[1]
    grid_rows, wide = orb.shape[1], orb.shape[2]
    group, prow, core = lax.axis_index("group"), lax.axis_index("prow"), lax.axis_index("pcol")
    pos = jnp.where(prow % 2 == 0, prow // 2, n - 1 - prow // 2)
    right = (group, ring_index((pos + 1) % n, n), core)
    left = (group, ring_index((pos + n - 1) % n, n), core)
    sibling = (group, prow, 1 - core)
    mine = pl.ds(pl.multiple_of(core * pts, pts), pts)
    theirs = pl.ds(pl.multiple_of((1 - core) * pts, pts), pts)
    side = (pl.ds(0, pts), pl.ds(pts, pts))

    def remote(src, dst, send, recv, device):
        return pltpu.make_async_remote_copy(
            src_ref=src, dst_ref=dst, send_sem=send, recv_sem=recv, device_id=device, device_id_type=MESH
        )

    def hop(way, s, c):
        static_first = isinstance(s, int) and s == 0
        static_last = isinstance(s, int) and s == last - 1
        src = rows.at[c, mine] if static_first else blocks.at[s, c, side[way]]
        dst = blocks.at[s + 1, c, side[0] if static_last else side[way]]
        return remote(
            src, dst, ring_send.at[way, s, c], ring_recv.at[way, s + 1, c], right if way == 0 else left
        )

    def row_copy(c):
        return remote(rows.at[c, mine], rows.at[c, mine], row_send.at[c], row_recv.at[c], sibling)

    def row_arrival(c):
        return remote(rows.at[c, theirs], rows.at[c, theirs], row_send.at[c], row_recv.at[c], sibling)

    def blk_copy(s, at_last=False):
        far = pl.ds((1 - core) * HALF, HALF)
        if at_last:
            return remote(
                blocks.at[s, far, side[0]], sib_blocks.at[s, :, side[0]], blk_send.at[s], blk_recv.at[s], sibling
            )
        return remote(blocks.at[s, far], sib_blocks.at[s], blk_send.at[s], blk_recv.at[s], sibling)

    def scr_copy(s, narrow=False):
        if narrow:
            return remote(
                scr.at[s, :, side[0]], sib_scr.at[s, :, side[0]], scr_send.at[s], scr_recv.at[s], sibling
            )
        return remote(scr.at[s], sib_scr.at[s], scr_send.at[s], scr_recv.at[s], sibling)

    def kernel_columns(index):
        return ker32[pl.ds(index, out_ref.shape[0], stride=n), :]

    order = (0, 2, 1, 3)
    loads = [
        pltpu.make_async_copy(orb_hbm.at[:, pl.ds(c * wide, wide)], orb.at[c], orb_sem.at[c]) for c in range(CH)
    ]
    pts_load = pltpu.make_async_copy(pts_hbm, pts_ref, pts_sem)
    pts_load.start()
    for c in order:
        loads[c].start()
    ker_load = pltpu.make_async_copy(ker_hbm, ker, ker_sem)
    ker_load.start()

    barrier = pltpu.get_barrier_semaphore()
    for device in (left, right, sibling):
        pl.semaphore_signal(barrier, inc=1, device_id=device, device_id_type=MESH)

    pts_load.wait()
    wanted = jnp.transpose(jnp.broadcast_to(pts_ref[...], (pts, pts)))
    wanted = jnp.concatenate([wanted] * (grid_rows // pts), axis=1)
    hot = (wanted == lax.broadcasted_iota(jnp.int32, (pts, grid_rows), 1)).astype(jnp.float32).astype(jnp.bfloat16)

    for k, c in enumerate(order):
        loads[c].wait()
        rows[c, mine] = dot(hot, orb[c]).astype(jnp.bfloat16)
        if k == 0:
            pl.semaphore_wait(barrier, 3)
        hop(0 if c < HALF else 1, 0, c).start()
        row_copy(c).start()
    for c in range(HALF):
        hop(0, 0, c + HALF).start()
        hop(1, 0, c).start()

    ker_load.wait()
    ker32[...] = ker[...].astype(jnp.float32).reshape(ker32.shape)

    for c in range(CH):
        row_arrival(c).wait_recv()
    density = dot_t(rows[0], rows[0, mine])
    for c in range(1, CH):
        density += dot_t(rows[c], rows[c, mine])
    screened = (kernel_columns(prow) * density).astype(jnp.bfloat16)
    scr[0, :, side[0]] = screened
    scr_copy(0, True).start()
    for i in range(HALF):
        acc[i] = dot(screened, rows[core * HALF + i, mine])

    def late(s):
        scr_copy(s).wait_recv()
        blk_copy(s).wait_recv()
        for i in range(HALF):
            acc[i] += dot(sib_scr[s], sib_blocks[s, i])

    def late_first():
        scr_copy(0, True).wait_recv()
        for i in range(HALF):
            acc[i] += dot(sib_scr[0, :, side[0]], rows[core * HALF + i, theirs])

    def step(s):
        for k in range(CH):
            for way in (0, 1):
                c = (k + way * HALF) % CH
                hop(way, s - 1, c).wait_recv()
                if not isinstance(s, int) or s < last - 1 or k < HALF:
                    hop(way, s, c).start()
        blk_copy(s).start()
        density = dot_t(rows[0], blocks[s, 0])
        for c in range(1, CH):
            density += dot_t(rows[c], blocks[s, c])
        from_left = kernel_columns(ring_index((pos + n - s) % n, n))
        from_right = kernel_columns(ring_index((pos + s) % n, n))
        screened = (jnp.concatenate([from_left, from_right], axis=1) * density).astype(jnp.bfloat16)
        scr[s] = screened
        scr_copy(s).start()
        for i in range(HALF):
            acc[i] += dot(screened, blocks[s, core * HALF + i])

    step(1)
    late_first()

    if last == 4:
        step(2)
        late(1)
    else:

        @pl.loop(2, last - 1)
        def _(s):
            step(s)
            late(s - 1)

    step(last - 1)
    late(last - 2)

    far = side[0]
    for k in range(HALF):
        hop(0, last - 1, k).wait_recv()
        hop(1, last - 1, k + HALF).wait_recv()
        part = dot_t(rows[k], blocks[last, k, far]) + dot_t(rows[k + HALF], blocks[last, k + HALF, far])
        density = part if k == 0 else density + part
    blk_copy(last, True).start()
    screened = (kernel_columns(ring_index((pos + last) % n, n)) * density).astype(jnp.bfloat16)
    scr[last, :, far] = screened
    scr_copy(last, True).start()
    late(last - 1)
    for i in range(HALF):
        acc[i] += dot(screened, blocks[last, core * HALF + i, far])
    blk_copy(last, True).wait_recv()
    scr_copy(last, True).wait_recv()
    for i in range(HALF):
        total = acc[i] + dot(sib_scr[last, :, far], sib_blocks[last, i, far])
        out_ref[:, pl.ds(i * wide, wide)] = total.astype(out_ref.dtype)

    for c in range(CH):
        row_copy(c).wait_send()
        for way in (0, 1):
            hop(way, 0, c).wait_send()
            hop(way, 1, c).wait_send()

    def drain(s):
        for c in range(CH):
            for way in (0, 1):
                hop(way, s, c).wait_send()

    if last == 4:
        drain(2)
    else:
        pl.loop(2, last - 1)(drain)
    for k in range(HALF):
        hop(0, last - 1, k).wait_send()
        hop(1, last - 1, k + HALF).wait_send()
    scr_copy(0, True).wait_send()
    scr_copy(last, True).wait_send()
    blk_copy(last, True).wait_send()

    def drain_pair(s):
        scr_copy(s).wait_send()
        blk_copy(s).wait_send()

    if last == 4:
        for s in range(1, last):
            drain_pair(s)
    else:
        pl.loop(1, last)(drain_pair)


def shards(n, orbitals, points, kernel):
    grid_rows, nocc = orbitals.shape
    pts = points.shape[0]
    row_total = kernel.shape[0]
    wide = nocc // CH
    slots = n // 2 + 1
    bf16, f32 = jnp.bfloat16, jnp.float32
    dma = pltpu.SemaphoreType.DMA
    scratch = [
        pltpu.VMEM((1, pts), jnp.int32),
        pltpu.VMEM((CH, grid_rows, wide), bf16),
        pltpu.VMEM((row_total, n, pts), bf16),
        pltpu.VMEM((row_total * n, pts), f32),
        pltpu.VMEM((CH, row_total, wide), bf16),
        pltpu.VMEM((slots, CH, 2 * pts, wide), bf16),
        pltpu.VMEM((slots, HALF, 2 * pts, wide), bf16),
        pltpu.VMEM((slots, row_total, 2 * pts), bf16),
        pltpu.VMEM((slots, row_total, 2 * pts), bf16),
        pltpu.VMEM((HALF, row_total, wide), f32),
        dma,
        dma((CH,)),
        dma,
        dma((CH,)),
        dma((CH,)),
        dma((2, slots, CH)),
        dma((2, slots, CH)),
        dma((slots,)),
        dma((slots,)),
        dma((slots,)),
        dma((slots,)),
    ]
    flops = 4 * row_total * n * pts * nocc
    return pl.pallas_call(
        functools.partial(body, n),
        out_shape=pltpu.VMEM((row_total, nocc // 2), bf16),
        in_specs=[
            pl.BlockSpec(memory_space=pl.ANY),
            pl.BlockSpec(memory_space=pl.ANY),
            pl.BlockSpec(memory_space=pl.ANY),
        ],
        out_specs=pl.BlockSpec(memory_space=pltpu.VMEM),
        scratch_shapes=scratch,
        compiler_params=pltpu.CompilerParams(
            collective_id=0, has_side_effects=True, vmem_limit_bytes=60 * 2**20
        ),
        cost_estimate=pl.CostEstimate(flops=flops, bytes_accessed=orbitals.size * 2, transcendentals=0),
    )(orbitals, points.reshape(1, pts), kernel.reshape(row_total, n, pts))


def solution(mesh):
    in_specs = (
        P(("group", "prow", "pcol"), None),
        P(("group", "prow", "pcol")),
        P(("group", "prow"), None, "pcol", None),
    )
    out_specs = P(("group", "prow"), "pcol")
    return jax.shard_map(
        functools.partial(shards, mesh.shape["prow"]),
        mesh=mesh, in_specs=in_specs, out_specs=out_specs, check_vma=False,
    )
```

```python
import functools

import jax
import jax.numpy as jnp
from jax import lax
from jax.experimental import pallas as pl
from jax.experimental.pallas import tpu as pltpu
from jax.sharding import PartitionSpec as P

MESH = pl.DeviceIdType.MESH
CH = 4
HALF = CH // 2


def ring_index(pos, n):
    return jnp.where(pos < n // 2, 2 * pos, 2 * (n - 1 - pos) + 1)


def dot(a, b):
    return jnp.dot(a, b, preferred_element_type=jnp.float32)


def dot_t(a, b):
    return lax.dot_general(a, b, (((1,), (1,)), ((), ())), preferred_element_type=jnp.float32)


def body(
    n, orb_hbm, pts_hbm, ker_hbm, out_ref,
    pts_ref, orb, ker, ker32, rows, blocks, sib_blocks, scr, sib_scr, acc,
    pts_sem, orb_sem, ker_sem, row_send, row_recv, ring_send, ring_recv, blk_send, blk_recv, scr_send, scr_recv,
):
    last = n // 2
    pts = pts_ref.shape[1]
    grid_rows, wide = orb.shape[1], orb.shape[2]
    group, prow, core = lax.axis_index("group"), lax.axis_index("prow"), lax.axis_index("pcol")
    pos = jnp.where(prow % 2 == 0, prow // 2, n - 1 - prow // 2)
    right = (group, ring_index((pos + 1) % n, n), core)
    left = (group, ring_index((pos + n - 1) % n, n), core)
    sibling = (group, prow, 1 - core)
    mine = pl.ds(pl.multiple_of(core * pts, pts), pts)
    theirs = pl.ds(pl.multiple_of((1 - core) * pts, pts), pts)
    side = (pl.ds(0, pts), pl.ds(pts, pts))

    def remote(src, dst, send, recv, device):
        return pltpu.make_async_remote_copy(
            src_ref=src, dst_ref=dst, send_sem=send, recv_sem=recv, device_id=device, device_id_type=MESH
        )

    def hop(way, s, c):
        static_first = isinstance(s, int) and s == 0
        static_last = isinstance(s, int) and s == last - 1
        src = rows.at[c, mine] if static_first else blocks.at[s, c, side[way]]
        dst = blocks.at[s + 1, c, side[0] if static_last else side[way]]
        return remote(
            src, dst, ring_send.at[way, s, c], ring_recv.at[way, s + 1, c], right if way == 0 else left
        )

    def row_copy(c):
        return remote(rows.at[c, mine], rows.at[c, mine], row_send.at[c], row_recv.at[c], sibling)

    def row_arrival(c):
        return remote(rows.at[c, theirs], rows.at[c, theirs], row_send.at[c], row_recv.at[c], sibling)

    def blk_copy(s, at_last=False):
        far = pl.ds((1 - core) * HALF, HALF)
        if at_last:
            return remote(
                blocks.at[s, far, side[0]], sib_blocks.at[s, :, side[0]], blk_send.at[s], blk_recv.at[s], sibling
            )
        return remote(blocks.at[s, far], sib_blocks.at[s], blk_send.at[s], blk_recv.at[s], sibling)

    def scr_copy(s, narrow=False):
        if narrow:
            return remote(
                scr.at[s, :, side[0]], sib_scr.at[s, :, side[0]], scr_send.at[s], scr_recv.at[s], sibling
            )
        return remote(scr.at[s], sib_scr.at[s], scr_send.at[s], scr_recv.at[s], sibling)

    def kernel_columns(index):
        return ker32[pl.ds(index, out_ref.shape[0], stride=n), :]

    order = (0, 2, 1, 3)
    loads = [
        pltpu.make_async_copy(orb_hbm.at[:, pl.ds(c * wide, wide)], orb.at[c], orb_sem.at[c]) for c in range(CH)
    ]
    pts_load = pltpu.make_async_copy(pts_hbm, pts_ref, pts_sem)
    pts_load.start()
    for c in order:
        loads[c].start()
    ker_load = pltpu.make_async_copy(ker_hbm, ker, ker_sem)
    ker_load.start()

    barrier = pltpu.get_barrier_semaphore()
    for device in (left, right, sibling):
        pl.semaphore_signal(barrier, inc=1, device_id=device, device_id_type=MESH)

    pts_load.wait()
    wanted = jnp.transpose(jnp.broadcast_to(pts_ref[...], (pts, pts)))
    wanted = jnp.concatenate([wanted] * (grid_rows // pts), axis=1)
    hot = (wanted == lax.broadcasted_iota(jnp.int32, (pts, grid_rows), 1)).astype(jnp.float32).astype(jnp.bfloat16)

    for k, c in enumerate(order):
        loads[c].wait()
        rows[c, mine] = dot(hot, orb[c]).astype(jnp.bfloat16)
        if k == 0:
            pl.semaphore_wait(barrier, 3)
        hop(0 if c < HALF else 1, 0, c).start()
        row_copy(c).start()
    for c in range(HALF):
        hop(0, 0, c + HALF).start()
        hop(1, 0, c).start()

    ker_load.wait()
    ker32[pl.ds(0, ker.shape[0] * n), :] = ker[...].astype(jnp.float32).reshape(ker.shape[0] * n, pts)

    for c in range(CH):
        row_arrival(c).wait_recv()
    density = dot_t(rows[0], rows[0, mine])
    for c in range(1, CH):
        density += dot_t(rows[c], rows[c, mine])
    screened = (kernel_columns(prow) * density).astype(jnp.bfloat16)
    scr[0, :, side[0]] = screened
    scr_copy(0, True).start()
    for i in range(HALF):
        acc[i] = dot(screened, rows[core * HALF + i, mine])

    def late(s):
        scr_copy(s).wait_recv()
        blk_copy(s).wait_recv()
        for i in range(HALF):
            acc[i] += dot(sib_scr[s], sib_blocks[s, i])

    def late_first():
        scr_copy(0, True).wait_recv()
        for i in range(HALF):
            acc[i] += dot(sib_scr[0, :, side[0]], rows[core * HALF + i, theirs])

    def step(s):
        for k in range(CH):
            for way in (0, 1):
                c = (k + way * HALF) % CH
                hop(way, s - 1, c).wait_recv()
                if not isinstance(s, int) or s < last - 1 or k < HALF:
                    hop(way, s, c).start()
        blk_copy(s).start()
        density = dot_t(rows[0], blocks[s, 0])
        for c in range(1, CH):
            density += dot_t(rows[c], blocks[s, c])
        from_left = kernel_columns(ring_index((pos + n - s) % n, n))
        from_right = kernel_columns(ring_index((pos + s) % n, n))
        screened = (jnp.concatenate([from_left, from_right], axis=1) * density).astype(jnp.bfloat16)
        scr[s] = screened
        scr_copy(s).start()
        for i in range(HALF):
            acc[i] += dot(screened, blocks[s, core * HALF + i])

    step(1)
    late_first()

    if last == 4:
        step(2)
        late(1)
    else:

        @pl.loop(2, last - 1)
        def _(s):
            step(s)
            late(s - 1)

    step(last - 1)
    late(last - 2)

    far = side[0]
    for k in range(HALF):
        hop(0, last - 1, k).wait_recv()
        hop(1, last - 1, k + HALF).wait_recv()
        part = dot_t(rows[k], blocks[last, k, far]) + dot_t(rows[k + HALF], blocks[last, k + HALF, far])
        density = part if k == 0 else density + part
    blk_copy(last, True).start()
    screened = (kernel_columns(ring_index((pos + last) % n, n)) * density).astype(jnp.bfloat16)
    scr[last, :, far] = screened
    scr_copy(last, True).start()
    late(last - 1)
    for i in range(HALF):
        acc[i] += dot(screened, blocks[last, core * HALF + i, far])
    blk_copy(last, True).wait_recv()
    scr_copy(last, True).wait_recv()
    for i in range(HALF):
        total = acc[i] + dot(sib_scr[last, :, far], sib_blocks[last, i, far])
        out_ref[:, pl.ds(i * wide, wide)] = total.astype(out_ref.dtype)

    for c in range(CH):
        row_copy(c).wait_send()
        for way in (0, 1):
            hop(way, 0, c).wait_send()
            hop(way, 1, c).wait_send()

    def drain(s):
        for c in range(CH):
            for way in (0, 1):
                hop(way, s, c).wait_send()

    if last == 4:
        drain(2)
    else:
        pl.loop(2, last - 1)(drain)
    for k in range(HALF):
        hop(0, last - 1, k).wait_send()
        hop(1, last - 1, k + HALF).wait_send()
    scr_copy(0, True).wait_send()
    scr_copy(last, True).wait_send()
    blk_copy(last, True).wait_send()

    def drain_pair(s):
        scr_copy(s).wait_send()
        blk_copy(s).wait_send()

    if last == 4:
        for s in range(1, last):
            drain_pair(s)
    else:
        pl.loop(1, last)(drain_pair)


def shards(n, orbitals, points, kernel):
    grid_rows, nocc = orbitals.shape
    pts = points.shape[0]
    row_total = kernel.shape[0]
    wide = nocc // CH
    slots = n // 2 + 1
    bf16, f32 = jnp.bfloat16, jnp.float32
    dma = pltpu.SemaphoreType.DMA
    scratch = [
        pltpu.VMEM((1, pts), jnp.int32),
        pltpu.VMEM((CH, grid_rows, wide), bf16),
        pltpu.VMEM((row_total, n, pts), bf16),
        pltpu.VMEM(((row_total + 1) * n, pts), f32),
        pltpu.VMEM((CH, row_total, wide), bf16),
        pltpu.VMEM((slots, CH, 2 * pts, wide), bf16),
        pltpu.VMEM((slots, HALF, 2 * pts, wide), bf16),
        pltpu.VMEM((slots, row_total, 2 * pts), bf16),
        pltpu.VMEM((slots, row_total, 2 * pts), bf16),
        pltpu.VMEM((HALF, row_total, wide), f32),
        dma,
        dma((CH,)),
        dma,
        dma((CH,)),
        dma((CH,)),
        dma((2, slots, CH)),
        dma((2, slots, CH)),
        dma((slots,)),
        dma((slots,)),
        dma((slots,)),
        dma((slots,)),
    ]
    flops = 4 * row_total * n * pts * nocc
    return pl.pallas_call(
        functools.partial(body, n),
        out_shape=pltpu.VMEM((row_total, nocc // 2), bf16),
        in_specs=[
            pl.BlockSpec(memory_space=pl.ANY),
            pl.BlockSpec(memory_space=pl.ANY),
            pl.BlockSpec(memory_space=pl.ANY),
        ],
        out_specs=pl.BlockSpec(memory_space=pltpu.VMEM),
        scratch_shapes=scratch,
        compiler_params=pltpu.CompilerParams(
            collective_id=0, has_side_effects=True, vmem_limit_bytes=60 * 2**20
        ),
        cost_estimate=pl.CostEstimate(flops=flops, bytes_accessed=orbitals.size * 2, transcendentals=0),
    )(orbitals, points.reshape(1, pts), kernel.reshape(row_total, n, pts))


def solution(mesh):
    in_specs = (
        P(("group", "prow", "pcol"), None),
        P(("group", "prow", "pcol")),
        P(("group", "prow"), None, "pcol", None),
    )
    out_specs = P(("group", "prow"), "pcol")
    return jax.shard_map(
        functools.partial(shards, mesh.shape["prow"]),
        mesh=mesh, in_specs=in_specs, out_specs=out_specs, check_vma=False,
    )
```

```python
import functools

import jax
import jax.numpy as jnp
from jax import lax
from jax.experimental import pallas as pl
from jax.experimental.pallas import tpu as pltpu
from jax.sharding import PartitionSpec as P

MESH = pl.DeviceIdType.MESH
CH = 4
HALF = CH // 2


def ring_index(pos, n):
    return jnp.where(pos < n // 2, 2 * pos, 2 * (n - 1 - pos) + 1)


def dot(a, b):
    return jnp.dot(a, b, preferred_element_type=jnp.float32)


def dot_t(a, b):
    return lax.dot_general(a, b, (((1,), (1,)), ((), ())), preferred_element_type=jnp.float32)


def body(
    n, orb_hbm, pts_hbm, ker_hbm, out_ref, both_ref, vals_ref,
    pts_ref, orb, ker, ker32, rows, blocks, sib_blocks, scr, sib_scr,
    pts_sem, orb_sem, ker_sem, row_send, row_recv, ring_send, ring_recv, blk_send, blk_recv, scr_send, scr_recv,
):
    last = n // 2
    pts = pts_ref.shape[1]
    grid_rows, wide = orb.shape[1], orb.shape[2]
    group, prow, core = lax.axis_index("group"), lax.axis_index("prow"), lax.axis_index("pcol")
    pos = jnp.where(prow % 2 == 0, prow // 2, n - 1 - prow // 2)
    right = (group, ring_index((pos + 1) % n, n), core)
    left = (group, ring_index((pos + n - 1) % n, n), core)
    sibling = (group, prow, 1 - core)
    mine = pl.ds(pl.multiple_of(core * pts, pts), pts)
    theirs = pl.ds(pl.multiple_of((1 - core) * pts, pts), pts)
    side = (pl.ds(0, pts), pl.ds(pts, pts))

    def remote(src, dst, send, recv, device):
        return pltpu.make_async_remote_copy(
            src_ref=src, dst_ref=dst, send_sem=send, recv_sem=recv, device_id=device, device_id_type=MESH
        )

    def hop(way, s, c):
        static_first = isinstance(s, int) and s == 0
        static_last = isinstance(s, int) and s == last - 1
        src = rows.at[c, mine] if static_first else blocks.at[s, c, side[way]]
        dst = blocks.at[s + 1, c, side[0] if static_last else side[way]]
        return remote(
            src, dst, ring_send.at[way, s, c], ring_recv.at[way, s + 1, c], right if way == 0 else left
        )

    def row_copy(c):
        return remote(rows.at[c, mine], rows.at[c, mine], row_send.at[c], row_recv.at[c], sibling)

    def row_arrival(c):
        return remote(rows.at[c, theirs], rows.at[c, theirs], row_send.at[c], row_recv.at[c], sibling)

    def blk_copy(s, at_last=False):
        far = pl.ds((1 - core) * HALF, HALF)
        if at_last:
            return remote(
                blocks.at[s, far, side[0]], sib_blocks.at[s, :, side[0]], blk_send.at[s], blk_recv.at[s], sibling
            )
        return remote(blocks.at[s, far], sib_blocks.at[s], blk_send.at[s], blk_recv.at[s], sibling)

    def last_copy(i):
        return remote(
            blocks.at[last, (1 - core) * HALF + i, side[0]], vals_ref.at[pl.ds(pts, pts), pl.ds(i * wide, wide)],
            blk_send.at[last - last * i], blk_recv.at[last - last * i], sibling,
        )

    last_scr = remote(
        scr.at[last, :, side[0]], both_ref.at[:, pl.ds(pts, pts)], scr_send.at[last], scr_recv.at[last], sibling
    )

    def scr_copy(s, narrow=False):
        if narrow:
            return remote(
                scr.at[s, :, side[0]], sib_scr.at[s, :, side[0]], scr_send.at[s], scr_recv.at[s], sibling
            )
        return remote(scr.at[s], sib_scr.at[s], scr_send.at[s], scr_recv.at[s], sibling)

    def kernel_columns(index):
        return ker32[pl.ds(index, out_ref.shape[0], stride=n), :]

    order = (0, 2, 1, 3)
    loads = [
        pltpu.make_async_copy(orb_hbm.at[:, pl.ds(c * wide, wide)], orb.at[c], orb_sem.at[c]) for c in range(CH)
    ]
    pts_load = pltpu.make_async_copy(pts_hbm, pts_ref, pts_sem)
    pts_load.start()
    for c in order:
        loads[c].start()
    ker_load = pltpu.make_async_copy(ker_hbm, ker, ker_sem)
    ker_load.start()

    barrier = pltpu.get_barrier_semaphore()
    for device in (left, right, sibling):
        pl.semaphore_signal(barrier, inc=1, device_id=device, device_id_type=MESH)

    pts_load.wait()
    wanted = jnp.transpose(jnp.broadcast_to(pts_ref[...], (pts, pts)))
    wanted = jnp.concatenate([wanted] * (grid_rows // pts), axis=1)
    hot = (wanted == lax.broadcasted_iota(jnp.int32, (pts, grid_rows), 1)).astype(jnp.float32).astype(jnp.bfloat16)

    for k, c in enumerate(order):
        loads[c].wait()
        rows[c, mine] = dot(hot, orb[c]).astype(jnp.bfloat16)
        if k == 0:
            pl.semaphore_wait(barrier, 3)
        hop(0 if c < HALF else 1, 0, c).start()
        row_copy(c).start()
    for c in range(HALF):
        hop(0, 0, c + HALF).start()
        hop(1, 0, c).start()

    ker_load.wait()
    ker32[pl.ds(0, ker.shape[0] * n), :] = ker[...].astype(jnp.float32).reshape(ker.shape[0] * n, pts)

    for c in range(CH):
        row_arrival(c).wait_recv()
    density = dot_t(rows[0], rows[0, mine])
    for c in range(1, CH):
        density += dot_t(rows[c], rows[c, mine])
    screened = (kernel_columns(prow) * density).astype(jnp.bfloat16)
    scr[0, :, side[0]] = screened
    scr_copy(0, True).start()
    for i in range(HALF):
        out_ref[:, pl.ds(i * wide, wide)] = dot(screened, rows[core * HALF + i, mine])

    def late(s):
        scr_copy(s).wait_recv()
        blk_copy(s).wait_recv()
        for i in range(HALF):
            out_ref[:, pl.ds(i * wide, wide)] += dot(sib_scr[s], sib_blocks[s, i])

    def late_first():
        scr_copy(0, True).wait_recv()
        for i in range(HALF):
            out_ref[:, pl.ds(i * wide, wide)] += dot(sib_scr[0, :, side[0]], rows[core * HALF + i, theirs])

    def step(s):
        for k in range(CH):
            for way in (0, 1):
                c = (k + way * HALF) % CH
                hop(way, s - 1, c).wait_recv()
                if not isinstance(s, int) or s < last - 1 or k < HALF:
                    hop(way, s, c).start()
        blk_copy(s).start()
        density = dot_t(rows[0], blocks[s, 0])
        for c in range(1, CH):
            density += dot_t(rows[c], blocks[s, c])
        from_left = kernel_columns(ring_index((pos + n - s) % n, n))
        from_right = kernel_columns(ring_index((pos + s) % n, n))
        screened = (jnp.concatenate([from_left, from_right], axis=1) * density).astype(jnp.bfloat16)
        scr[s] = screened
        scr_copy(s).start()
        for i in range(HALF):
            out_ref[:, pl.ds(i * wide, wide)] += dot(screened, blocks[s, core * HALF + i])

    step(1)
    late_first()

    if last == 4:
        step(2)
        late(1)
    else:

        @pl.loop(2, last - 1)
        def _(s):
            step(s)
            late(s - 1)

    step(last - 1)
    late(last - 2)

    def drain(s):
        for c in range(CH):
            for way in (0, 1):
                hop(way, s, c).wait_send()

    def drain_pair(s):
        scr_copy(s).wait_send()
        blk_copy(s).wait_send()

    for c in range(CH):
        row_copy(c).wait_send()
    drain(0)
    drain(1)
    scr_copy(0, True).wait_send()
    if last == 4:
        drain_pair(1)
        drain_pair(2)
    else:
        pl.loop(2, last - 2)(drain)
        pl.loop(1, last - 1)(drain_pair)

    far = side[0]
    for k in range(HALF):
        hop(0, last - 1, k).wait_recv()
        hop(1, last - 1, k + HALF).wait_recv()
        part = dot_t(rows[k], blocks[last, k, far]) + dot_t(rows[k + HALF], blocks[last, k + HALF, far])
        density = part if k == 0 else density + part
    for i in range(HALF):
        last_copy(i).start()
    screened = (kernel_columns(ring_index((pos + last) % n, n)) * density).astype(jnp.bfloat16)
    scr[last, :, far] = screened
    last_scr.start()
    late(last - 1)
    both_ref[:, pl.ds(0, pts)] = screened
    for i in range(HALF):
        vals_ref[pl.ds(0, pts), pl.ds(i * wide, wide)] = blocks[last, core * HALF + i, far]
    drain(last - 2)
    for k in range(HALF):
        hop(0, last - 1, k).wait_send()
        hop(1, last - 1, k + HALF).wait_send()
    drain_pair(last - 1)
    for i in range(HALF):
        last_copy(i).wait()
    last_scr.wait()


def shards(n, orbitals, points, kernel):
    grid_rows, nocc = orbitals.shape
    pts = points.shape[0]
    row_total = kernel.shape[0]
    wide = nocc // CH
    slots = n // 2 + 1
    bf16, f32 = jnp.bfloat16, jnp.float32
    dma = pltpu.SemaphoreType.DMA
    scratch = [
        pltpu.VMEM((1, pts), jnp.int32),
        pltpu.VMEM((CH, grid_rows, wide), bf16),
        pltpu.VMEM((row_total, n, pts), bf16),
        pltpu.VMEM(((row_total + 1) * n, pts), f32),
        pltpu.VMEM((CH, row_total, wide), bf16),
        pltpu.VMEM((slots, CH, 2 * pts, wide), bf16),
        pltpu.VMEM((slots, HALF, 2 * pts, wide), bf16),
        pltpu.VMEM((slots, row_total, 2 * pts), bf16),
        pltpu.VMEM((slots, row_total, 2 * pts), bf16),
        dma,
        dma((CH,)),
        dma,
        dma((CH,)),
        dma((CH,)),
        dma((2, slots, CH)),
        dma((2, slots, CH)),
        dma((slots,)),
        dma((slots,)),
        dma((slots,)),
        dma((slots,)),
    ]
    flops = 4 * row_total * n * pts * nocc
    total, screened, values = pl.pallas_call(
        functools.partial(body, n),
        out_shape=(
            pltpu.VMEM((row_total, nocc // 2), f32),
            pltpu.VMEM((row_total, 2 * pts), bf16),
            pltpu.VMEM((2 * pts, nocc // 2), bf16),
        ),
        in_specs=[
            pl.BlockSpec(memory_space=pl.ANY),
            pl.BlockSpec(memory_space=pl.ANY),
            pl.BlockSpec(memory_space=pl.ANY),
        ],
        out_specs=(pl.BlockSpec(memory_space=pltpu.VMEM),) * 3,
        scratch_shapes=scratch,
        compiler_params=pltpu.CompilerParams(
            collective_id=0, has_side_effects=True, vmem_limit_bytes=60 * 2**20
        ),
        cost_estimate=pl.CostEstimate(flops=flops, bytes_accessed=orbitals.size * 2, transcendentals=0),
    )(orbitals, points.reshape(1, pts), kernel.reshape(row_total, n, pts))
    return (total + dot(screened, values)).astype(bf16)


def solution(mesh):
    in_specs = (
        P(("group", "prow", "pcol"), None),
        P(("group", "prow", "pcol")),
        P(("group", "prow"), None, "pcol", None),
    )
    out_specs = P(("group", "prow"), "pcol")
    return jax.shard_map(
        functools.partial(shards, mesh.shape["prow"]),
        mesh=mesh, in_specs=in_specs, out_specs=out_specs, check_vma=False,
    )
```

```python
import functools

import jax
import jax.numpy as jnp
from jax import lax
from jax.experimental import pallas as pl
from jax.experimental.pallas import tpu as pltpu
from jax.sharding import PartitionSpec as P

MESH = pl.DeviceIdType.MESH
CH = 4
HALF = CH // 2


def ring_index(pos, n):
    return jnp.where(pos < n // 2, 2 * pos, 2 * (n - 1 - pos) + 1)


def dot(a, b):
    return jnp.dot(a, b, preferred_element_type=jnp.float32)


def dot_t(a, b):
    return lax.dot_general(a, b, (((1,), (1,)), ((), ())), preferred_element_type=jnp.float32)


def body(
    n, orb_hbm, pts_hbm, ker_hbm, out_ref,
    pts_ref, orb, ker, ker32, rows, blocks, sib_blocks, scr, sib_scr, acc,
    pts_sem, orb_sem, ker_sem, row_send, row_recv, ring_send, ring_recv, blk_send, blk_recv, scr_send, scr_recv,
):
    last = n // 2
    pts = pts_ref.shape[1]
    grid_rows, wide = orb.shape[1], orb.shape[2]
    group, prow, core = lax.axis_index("group"), lax.axis_index("prow"), lax.axis_index("pcol")
    pos = jnp.where(prow % 2 == 0, prow // 2, n - 1 - prow // 2)
    right = (group, ring_index((pos + 1) % n, n), core)
    left = (group, ring_index((pos + n - 1) % n, n), core)
    sibling = (group, prow, 1 - core)
    mine = pl.ds(pl.multiple_of(core * pts, pts), pts)
    theirs = pl.ds(pl.multiple_of((1 - core) * pts, pts), pts)
    side = (pl.ds(0, pts), pl.ds(pts, pts))

    def remote(src, dst, send, recv, device):
        return pltpu.make_async_remote_copy(
            src_ref=src, dst_ref=dst, send_sem=send, recv_sem=recv, device_id=device, device_id_type=MESH
        )

    def hop(way, s, c):
        static_first = isinstance(s, int) and s == 0
        static_last = isinstance(s, int) and s == last - 1
        src = rows.at[c, mine] if static_first else blocks.at[s, c, side[way]]
        dst = blocks.at[s + 1, c, side[0] if static_last else side[way]]
        return remote(
            src, dst, ring_send.at[way, s, c], ring_recv.at[way, s + 1, c], right if way == 0 else left
        )

    def row_copy(c):
        return remote(rows.at[c, mine], rows.at[c, mine], row_send.at[c], row_recv.at[c], sibling)

    def row_arrival(c):
        return remote(rows.at[c, theirs], rows.at[c, theirs], row_send.at[c], row_recv.at[c], sibling)

    def blk_copy(s, at_last=False):
        far = pl.ds((1 - core) * HALF, HALF)
        if at_last:
            return remote(
                blocks.at[s, far, side[0]], sib_blocks.at[s, :, side[0]], blk_send.at[s], blk_recv.at[s], sibling
            )
        return remote(blocks.at[s, far], sib_blocks.at[s], blk_send.at[s], blk_recv.at[s], sibling)

    def scr_copy(s, narrow=False):
        if narrow:
            return remote(
                scr.at[s, :, side[0]], sib_scr.at[s, :, side[0]], scr_send.at[s], scr_recv.at[s], sibling
            )
        return remote(scr.at[s], sib_scr.at[s], scr_send.at[s], scr_recv.at[s], sibling)

    def kernel_columns(index):
        return ker32[pl.ds(index, out_ref.shape[0], stride=n), :]

    order = (0, 2, 1, 3)
    loads = [
        pltpu.make_async_copy(orb_hbm.at[:, pl.ds(c * wide, wide)], orb.at[c], orb_sem.at[c]) for c in range(CH)
    ]
    pts_load = pltpu.make_async_copy(pts_hbm, pts_ref, pts_sem)
    pts_load.start()
    for k, c in enumerate(order):
        loads[c].start(priority=1 if k else 0)
    ker_load = pltpu.make_async_copy(ker_hbm, ker, ker_sem)
    ker_load.start(priority=1)

    barrier = pltpu.get_barrier_semaphore()
    for device in (left, right, sibling):
        pl.semaphore_signal(barrier, inc=1, device_id=device, device_id_type=MESH)

    pts_load.wait()
    wanted = jnp.transpose(jnp.broadcast_to(pts_ref[...], (pts, pts)))
    wanted = jnp.concatenate([wanted] * (grid_rows // pts), axis=1)
    hot = (wanted == lax.broadcasted_iota(jnp.int32, (pts, grid_rows), 1)).astype(jnp.float32).astype(jnp.bfloat16)

    for k, c in enumerate(order):
        loads[c].wait()
        rows[c, mine] = dot(hot, orb[c]).astype(jnp.bfloat16)
        if k == 0:
            pl.semaphore_wait(barrier, 3)
        hop(0 if c < HALF else 1, 0, c).start()
        row_copy(c).start()
    for c in range(HALF):
        hop(0, 0, c + HALF).start()
        hop(1, 0, c).start()

    ker_load.wait()
    ker32[pl.ds(0, ker.shape[0] * n), :] = ker[...].astype(jnp.float32).reshape(ker.shape[0] * n, pts)

    for c in range(CH):
        row_arrival(c).wait_recv()
    density = dot_t(rows[0], rows[0, mine])
    for c in range(1, CH):
        density += dot_t(rows[c], rows[c, mine])
    screened = (kernel_columns(prow) * density).astype(jnp.bfloat16)
    scr[0, :, side[0]] = screened
    scr_copy(0, True).start()
    for i in range(HALF):
        acc[i] = dot(screened, rows[core * HALF + i, mine])

    def late(s):
        scr_copy(s).wait_recv()
        blk_copy(s).wait_recv()
        for i in range(HALF):
            acc[i] += dot(sib_scr[s], sib_blocks[s, i])

    def late_first():
        scr_copy(0, True).wait_recv()
        for i in range(HALF):
            acc[i] += dot(sib_scr[0, :, side[0]], rows[core * HALF + i, theirs])

    def step(s):
        for k in range(CH):
            for way in (0, 1):
                c = (k + way * HALF) % CH
                hop(way, s - 1, c).wait_recv()
                if not isinstance(s, int) or s < last - 1 or k < HALF:
                    hop(way, s, c).start()
        blk_copy(s).start()
        density = dot_t(rows[0], blocks[s, 0])
        for c in range(1, CH):
            density += dot_t(rows[c], blocks[s, c])
        from_left = kernel_columns(ring_index((pos + n - s) % n, n))
        from_right = kernel_columns(ring_index((pos + s) % n, n))
        screened = (jnp.concatenate([from_left, from_right], axis=1) * density).astype(jnp.bfloat16)
        scr[s] = screened
        scr_copy(s).start()
        for i in range(HALF):
            acc[i] += dot(screened, blocks[s, core * HALF + i])

    step(1)
    late_first()

    if last == 4:
        step(2)
        late(1)
    else:

        @pl.loop(2, last - 1)
        def _(s):
            step(s)
            late(s - 1)

    step(last - 1)
    late(last - 2)

    far = side[0]
    for k in range(HALF):
        hop(0, last - 1, k).wait_recv()
        hop(1, last - 1, k + HALF).wait_recv()
        part = dot_t(rows[k], blocks[last, k, far]) + dot_t(rows[k + HALF], blocks[last, k + HALF, far])
        density = part if k == 0 else density + part
    blk_copy(last, True).start()
    screened = (kernel_columns(ring_index((pos + last) % n, n)) * density).astype(jnp.bfloat16)
    scr[last, :, far] = screened
    scr_copy(last, True).start()
    late(last - 1)
    for i in range(HALF):
        acc[i] += dot(screened, blocks[last, core * HALF + i, far])
    blk_copy(last, True).wait_recv()
    scr_copy(last, True).wait_recv()
    for i in range(HALF):
        total = acc[i] + dot(sib_scr[last, :, far], sib_blocks[last, i, far])
        out_ref[:, pl.ds(i * wide, wide)] = total.astype(out_ref.dtype)

    for c in range(CH):
        row_copy(c).wait_send()
        for way in (0, 1):
            hop(way, 0, c).wait_send()
            hop(way, 1, c).wait_send()

    def drain(s):
        for c in range(CH):
            for way in (0, 1):
                hop(way, s, c).wait_send()

    if last == 4:
        drain(2)
    else:
        pl.loop(2, last - 1)(drain)
    for k in range(HALF):
        hop(0, last - 1, k).wait_send()
        hop(1, last - 1, k + HALF).wait_send()
    scr_copy(0, True).wait_send()
    scr_copy(last, True).wait_send()
    blk_copy(last, True).wait_send()

    def drain_pair(s):
        scr_copy(s).wait_send()
        blk_copy(s).wait_send()

    if last == 4:
        for s in range(1, last):
            drain_pair(s)
    else:
        pl.loop(1, last)(drain_pair)


def shards(n, orbitals, points, kernel):
    grid_rows, nocc = orbitals.shape
    pts = points.shape[0]
    row_total = kernel.shape[0]
    wide = nocc // CH
    slots = n // 2 + 1
    bf16, f32 = jnp.bfloat16, jnp.float32
    dma = pltpu.SemaphoreType.DMA
    scratch = [
        pltpu.VMEM((1, pts), jnp.int32),
        pltpu.VMEM((CH, grid_rows, wide), bf16),
        pltpu.VMEM((row_total, n, pts), bf16),
        pltpu.VMEM(((row_total + 1) * n, pts), f32),
        pltpu.VMEM((CH, row_total, wide), bf16),
        pltpu.VMEM((slots, CH, 2 * pts, wide), bf16),
        pltpu.VMEM((slots, HALF, 2 * pts, wide), bf16),
        pltpu.VMEM((slots, row_total, 2 * pts), bf16),
        pltpu.VMEM((slots, row_total, 2 * pts), bf16),
        pltpu.VMEM((HALF, row_total, wide), f32),
        dma,
        dma((CH,)),
        dma,
        dma((CH,)),
        dma((CH,)),
        dma((2, slots, CH)),
        dma((2, slots, CH)),
        dma((slots,)),
        dma((slots,)),
        dma((slots,)),
        dma((slots,)),
    ]
    flops = 4 * row_total * n * pts * nocc
    return pl.pallas_call(
        functools.partial(body, n),
        out_shape=pltpu.VMEM((row_total, nocc // 2), bf16),
        in_specs=[
            pl.BlockSpec(memory_space=pl.ANY),
            pl.BlockSpec(memory_space=pl.ANY),
            pl.BlockSpec(memory_space=pl.ANY),
        ],
        out_specs=pl.BlockSpec(memory_space=pltpu.VMEM),
        scratch_shapes=scratch,
        compiler_params=pltpu.CompilerParams(
            collective_id=0, has_side_effects=True, vmem_limit_bytes=60 * 2**20
        ),
        cost_estimate=pl.CostEstimate(flops=flops, bytes_accessed=orbitals.size * 2, transcendentals=0),
    )(orbitals, points.reshape(1, pts), kernel.reshape(row_total, n, pts))


def solution(mesh):
    in_specs = (
        P(("group", "prow", "pcol"), None),
        P(("group", "prow", "pcol")),
        P(("group", "prow"), None, "pcol", None),
    )
    out_specs = P(("group", "prow"), "pcol")
    return jax.shard_map(
        functools.partial(shards, mesh.shape["prow"]),
        mesh=mesh, in_specs=in_specs, out_specs=out_specs, check_vma=False,
    )
```

```python
import functools

import jax
import jax.numpy as jnp
from jax import lax
from jax.experimental import pallas as pl
from jax.experimental.pallas import tpu as pltpu
from jax.sharding import PartitionSpec as P

MESH = pl.DeviceIdType.MESH
CH = 4
HALF = CH // 2


def ring_index(pos, n):
    return jnp.where(pos < n // 2, 2 * pos, 2 * (n - 1 - pos) + 1)


def dot(a, b):
    return jnp.dot(a, b, preferred_element_type=jnp.float32)


def dot_t(a, b):
    return lax.dot_general(a, b, (((1,), (1,)), ((), ())), preferred_element_type=jnp.float32)


def body(
    n, orb_hbm, pts_hbm, ker_hbm, out_ref,
    pts_ref, orb, ker, ker32, rows, blocks, sib_blocks, scr, sib_scr, acc,
    pts_sem, orb_sem, ker_sem, row_send, row_recv, ring_send, ring_recv, blk_send, blk_recv, scr_send, scr_recv,
):
    last = n // 2
    pts = pts_ref.shape[1]
    grid_rows, wide = orb.shape[1], orb.shape[2]
    group, prow, core = lax.axis_index("group"), lax.axis_index("prow"), lax.axis_index("pcol")
    pos = jnp.where(prow % 2 == 0, prow // 2, n - 1 - prow // 2)
    right = (group, ring_index((pos + 1) % n, n), core)
    left = (group, ring_index((pos + n - 1) % n, n), core)
    sibling = (group, prow, 1 - core)
    mine = pl.ds(pl.multiple_of(core * pts, pts), pts)
    theirs = pl.ds(pl.multiple_of((1 - core) * pts, pts), pts)
    side = (pl.ds(0, pts), pl.ds(pts, pts))

    def remote(src, dst, send, recv, device):
        return pltpu.make_async_remote_copy(
            src_ref=src, dst_ref=dst, send_sem=send, recv_sem=recv, device_id=device, device_id_type=MESH
        )

    def hop(way, s, c):
        static_first = isinstance(s, int) and s == 0
        static_last = isinstance(s, int) and s == last - 1
        src = rows.at[c, mine] if static_first else blocks.at[s, c, side[way]]
        dst = blocks.at[s + 1, c, side[0] if static_last else side[way]]
        return remote(
            src, dst, ring_send.at[way, s, c], ring_recv.at[way, s + 1, c], right if way == 0 else left
        )

    def row_copy(c):
        return remote(rows.at[c, mine], rows.at[c, mine], row_send.at[c], row_recv.at[c], sibling)

    def row_arrival(c):
        return remote(rows.at[c, theirs], rows.at[c, theirs], row_send.at[c], row_recv.at[c], sibling)

    def blk_copy(s, at_last=False):
        far = pl.ds((1 - core) * HALF, HALF)
        if at_last:
            return remote(
                blocks.at[s, far, side[0]], sib_blocks.at[s, :, side[0]], blk_send.at[s], blk_recv.at[s], sibling
            )
        return remote(blocks.at[s, far], sib_blocks.at[s], blk_send.at[s], blk_recv.at[s], sibling)

    def scr_copy(s, narrow=False):
        if narrow:
            return remote(
                scr.at[s, :, side[0]], sib_scr.at[s, :, side[0]], scr_send.at[s], scr_recv.at[s], sibling
            )
        return remote(scr.at[s], sib_scr.at[s], scr_send.at[s], scr_recv.at[s], sibling)

    def kernel_columns(index):
        return ker32[pl.ds(index, out_ref.shape[0], stride=n), :]

    order = (0, 2, 1, 3)
    loads = [
        pltpu.make_async_copy(orb_hbm.at[:, pl.ds(c * wide, wide)], orb.at[c], orb_sem.at[c]) for c in range(CH)
    ]
    pts_load = pltpu.make_async_copy(pts_hbm, pts_ref, pts_sem)
    pts_load.start()
    for k, c in enumerate(order):
        loads[c].start(priority=1 if k > 1 else 0)
    ker_load = pltpu.make_async_copy(ker_hbm, ker, ker_sem)
    ker_load.start(priority=1)

    barrier = pltpu.get_barrier_semaphore()
    for device in (left, right, sibling):
        pl.semaphore_signal(barrier, inc=1, device_id=device, device_id_type=MESH)

    pts_load.wait()
    wanted = jnp.transpose(jnp.broadcast_to(pts_ref[...], (pts, pts)))
    wanted = jnp.concatenate([wanted] * (grid_rows // pts), axis=1)
    hot = (wanted == lax.broadcasted_iota(jnp.int32, (pts, grid_rows), 1)).astype(jnp.float32).astype(jnp.bfloat16)

    for k, c in enumerate(order):
        loads[c].wait()
        rows[c, mine] = dot(hot, orb[c]).astype(jnp.bfloat16)
        if k == 0:
            pl.semaphore_wait(barrier, 3)
        hop(0 if c < HALF else 1, 0, c).start()
        row_copy(c).start()
    for c in range(HALF):
        hop(0, 0, c + HALF).start()
        hop(1, 0, c).start()

    ker_load.wait()
    ker32[pl.ds(0, ker.shape[0] * n), :] = ker[...].astype(jnp.float32).reshape(ker.shape[0] * n, pts)

    for c in range(CH):
        row_arrival(c).wait_recv()
    density = dot_t(rows[0], rows[0, mine])
    for c in range(1, CH):
        density += dot_t(rows[c], rows[c, mine])
    screened = (kernel_columns(prow) * density).astype(jnp.bfloat16)
    scr[0, :, side[0]] = screened
    scr_copy(0, True).start()
    for i in range(HALF):
        acc[i] = dot(screened, rows[core * HALF + i, mine])

    def late(s):
        scr_copy(s).wait_recv()
        blk_copy(s).wait_recv()
        for i in range(HALF):
            acc[i] += dot(sib_scr[s], sib_blocks[s, i])

    def late_first():
        scr_copy(0, True).wait_recv()
        for i in range(HALF):
            acc[i] += dot(sib_scr[0, :, side[0]], rows[core * HALF + i, theirs])

    def step(s):
        for k in range(CH):
            for way in (0, 1):
                c = (k + way * HALF) % CH
                hop(way, s - 1, c).wait_recv()
                if not isinstance(s, int) or s < last - 1 or k < HALF:
                    hop(way, s, c).start()
        blk_copy(s).start()
        density = dot_t(rows[0], blocks[s, 0])
        for c in range(1, CH):
            density += dot_t(rows[c], blocks[s, c])
        from_left = kernel_columns(ring_index((pos + n - s) % n, n))
        from_right = kernel_columns(ring_index((pos + s) % n, n))
        screened = (jnp.concatenate([from_left, from_right], axis=1) * density).astype(jnp.bfloat16)
        scr[s] = screened
        scr_copy(s).start()
        for i in range(HALF):
            acc[i] += dot(screened, blocks[s, core * HALF + i])

    step(1)
    late_first()

    if last == 4:
        step(2)
        late(1)
    else:

        @pl.loop(2, last - 1)
        def _(s):
            step(s)
            late(s - 1)

    step(last - 1)
    late(last - 2)

    far = side[0]
    for k in range(HALF):
        hop(0, last - 1, k).wait_recv()
        hop(1, last - 1, k + HALF).wait_recv()
        part = dot_t(rows[k], blocks[last, k, far]) + dot_t(rows[k + HALF], blocks[last, k + HALF, far])
        density = part if k == 0 else density + part
    blk_copy(last, True).start()
    screened = (kernel_columns(ring_index((pos + last) % n, n)) * density).astype(jnp.bfloat16)
    scr[last, :, far] = screened
    scr_copy(last, True).start()
    late(last - 1)
    for i in range(HALF):
        acc[i] += dot(screened, blocks[last, core * HALF + i, far])
    blk_copy(last, True).wait_recv()
    scr_copy(last, True).wait_recv()
    for i in range(HALF):
        total = acc[i] + dot(sib_scr[last, :, far], sib_blocks[last, i, far])
        out_ref[:, pl.ds(i * wide, wide)] = total.astype(out_ref.dtype)

    for c in range(CH):
        row_copy(c).wait_send()
        for way in (0, 1):
            hop(way, 0, c).wait_send()
            hop(way, 1, c).wait_send()

    def drain(s):
        for c in range(CH):
            for way in (0, 1):
                hop(way, s, c).wait_send()

    if last == 4:
        drain(2)
    else:
        pl.loop(2, last - 1)(drain)
    for k in range(HALF):
        hop(0, last - 1, k).wait_send()
        hop(1, last - 1, k + HALF).wait_send()
    scr_copy(0, True).wait_send()
    scr_copy(last, True).wait_send()
    blk_copy(last, True).wait_send()

    def drain_pair(s):
        scr_copy(s).wait_send()
        blk_copy(s).wait_send()

    if last == 4:
        for s in range(1, last):
            drain_pair(s)
    else:
        pl.loop(1, last)(drain_pair)


def shards(n, orbitals, points, kernel):
    grid_rows, nocc = orbitals.shape
    pts = points.shape[0]
    row_total = kernel.shape[0]
    wide = nocc // CH
    slots = n // 2 + 1
    bf16, f32 = jnp.bfloat16, jnp.float32
    dma = pltpu.SemaphoreType.DMA
    scratch = [
        pltpu.VMEM((1, pts), jnp.int32),
        pltpu.VMEM((CH, grid_rows, wide), bf16),
        pltpu.VMEM((row_total, n, pts), bf16),
        pltpu.VMEM(((row_total + 1) * n, pts), f32),
        pltpu.VMEM((CH, row_total, wide), bf16),
        pltpu.VMEM((slots, CH, 2 * pts, wide), bf16),
        pltpu.VMEM((slots, HALF, 2 * pts, wide), bf16),
        pltpu.VMEM((slots, row_total, 2 * pts), bf16),
        pltpu.VMEM((slots, row_total, 2 * pts), bf16),
        pltpu.VMEM((HALF, row_total, wide), f32),
        dma,
        dma((CH,)),
        dma,
        dma((CH,)),
        dma((CH,)),
        dma((2, slots, CH)),
        dma((2, slots, CH)),
        dma((slots,)),
        dma((slots,)),
        dma((slots,)),
        dma((slots,)),
    ]
    flops = 4 * row_total * n * pts * nocc
    return pl.pallas_call(
        functools.partial(body, n),
        out_shape=pltpu.VMEM((row_total, nocc // 2), bf16),
        in_specs=[
            pl.BlockSpec(memory_space=pl.ANY),
            pl.BlockSpec(memory_space=pl.ANY),
            pl.BlockSpec(memory_space=pl.ANY),
        ],
        out_specs=pl.BlockSpec(memory_space=pltpu.VMEM),
        scratch_shapes=scratch,
        compiler_params=pltpu.CompilerParams(
            collective_id=0, has_side_effects=True, vmem_limit_bytes=60 * 2**20
        ),
        cost_estimate=pl.CostEstimate(flops=flops, bytes_accessed=orbitals.size * 2, transcendentals=0),
    )(orbitals, points.reshape(1, pts), kernel.reshape(row_total, n, pts))


def solution(mesh):
    in_specs = (
        P(("group", "prow", "pcol"), None),
        P(("group", "prow", "pcol")),
        P(("group", "prow"), None, "pcol", None),
    )
    out_specs = P(("group", "prow"), "pcol")
    return jax.shard_map(
        functools.partial(shards, mesh.shape["prow"]),
        mesh=mesh, in_specs=in_specs, out_specs=out_specs, check_vma=False,
    )
```
